32 devices in a mesh: freq: 4 (over y, core), sky: 8 (over z, x).
Axes of the slice: x: 2, y: 2, z: 4, core: 2. Of those that a mesh axis runs over, the one named last changes fastest.
Arguments:
- sky_cube: bfloat16 [256, 256, 1024], P(None, 'sky', 'freq'), may hold values from -6 to 6
- weight_first: bfloat16 [3, 3, 1024, 256], P(None, None, 'freq'), may hold values from -0.0625 to 0.0625
- weight_second: bfloat16 [3, 3, 256, 256], replicated, may hold values from -0.125 to 0.125
- cotangent: bfloat16 [256, 256, 256], P('freq', 'sky'), may hold values from -0.0234375 to 0.0234375
Outputs:
- features: bfloat16 [256, 256, 256], P('freq', 'sky')
- grad_first: float32 [3, 3, 1024, 256], P(None, None, 'freq')
- grad_second: float32 [3, 3, 256, 256], replicated
The draws below stay inside these ranges and needn't reach their ends.
All inputs are finite; a program needn't handle non-finite values.
Results may differ from the reference program's by a relative error of at most 0.024.
Values may be sent and summed in bfloat16 or wider, within the bound.
A program may use at most 128 MiB of HBM per device.

```python
import jax
import jax.numpy as jnp

CIN = 1024
CH = 256
NCOL = 256
NROW = 256


def block_levels(rng, dims, pieces, smallest, top_value):
    def one(dim, parts):
        steps = jax.random.uniform(jax.random.fold_in(jax.random.fold_in(rng, 6), dim), (parts,), jnp.float32, smallest / len(pieces), top_value / len(pieces))
        return jnp.repeat(jnp.exp(steps), dims[dim] // parts).reshape((-1,) + (1,) * (len(dims) - dim - 1))

    factor_of = one(*pieces[0])
    for cut in pieces[1:]:
        factor_of = factor_of * one(*cut)
    return factor_of


def bell_draw(rng, dims, deviation, reach, shards=(), held_as=jnp.bfloat16):
    loudness = block_levels(rng, dims, shards, -0.22, 0.18) if shards else 1.0
    result = jax.random.normal(rng, dims, jnp.float32) * deviation * loudness
    return jnp.minimum(jnp.maximum(result, -reach), reach).astype(held_as)


def setup_inputs(seed: int = 0) -> dict:
    keys = jax.random.split(jax.random.key(seed), 5)
    return {
        "sky_cube": bell_draw(keys[0], (NCOL, NROW, CIN), 1.0, 6.0, ((1, 8), (2, 4))),
        "weight_first": bell_draw(keys[1], (3, 3, CIN, CH), (9 * CIN) ** -0.5, 0.0625, ((2, 4),)),
        "weight_second": bell_draw(keys[2], (3, 3, CH, CH), (9 * CH) ** -0.5, 0.125),
        "cotangent": bell_draw(keys[3], (NCOL, NROW, CH), (1.0 / (NCOL * NROW) ** 0.5), 0.0234375, ((0, 4), (1, 8))),
    }


def conv_taps(padded, kernel, col_count, row_count):
    total = jnp.zeros((col_count * row_count, kernel.shape[3]), jnp.float32)
    for tap_col in range(3):
        for tap_row in range(3):
            piece = padded[tap_col:tap_col + col_count, tap_row:tap_row + row_count].reshape(col_count * row_count, -1)
            total = total + jnp.dot(piece, kernel[tap_col, tap_row], preferred_element_type=jnp.float32)
    return total.reshape(col_count, row_count, kernel.shape[3])

def conv_back(padded, kernel, col_count, row_count):
    total = jnp.zeros((col_count * row_count, kernel.shape[2]), jnp.float32)
    for tap_col in range(3):
        for tap_row in range(3):
            piece = padded[2 - tap_col:2 - tap_col + col_count, 2 - tap_row:2 - tap_row + row_count].reshape(col_count * row_count, -1)
            total = total + jnp.dot(piece, kernel[tap_col, tap_row].T, preferred_element_type=jnp.float32)
    return total.reshape(col_count, row_count, kernel.shape[2])

def kernel_grad(padded, grads, col_count, row_count):
    flat = grads.reshape(col_count * row_count, -1)
    rows_out = []
    for tap_col in range(3):
        line = []
        for tap_row in range(3):
            piece = padded[tap_col:tap_col + col_count, tap_row:tap_row + row_count].reshape(col_count * row_count, -1)
            line.append(jnp.dot(piece.T, flat, preferred_element_type=jnp.float32))
        rows_out.append(jnp.stack(line))
    return jnp.stack(rows_out)

def pad_sky(field):
    return jnp.pad(field, ((1, 1), (1, 1), (0, 0)))

def reference(sky_cube, weight_first, weight_second, cotangent):
    cube_pad = pad_sky(sky_cube)
    pre = conv_taps(cube_pad, weight_first, NCOL, NROW)
    hidden = jax.nn.silu(pre).astype(jnp.bfloat16)
    hidden_pad = pad_sky(hidden)
    features = conv_taps(hidden_pad, weight_second, NCOL, NROW).astype(jnp.bfloat16)
    back = conv_back(pad_sky(cotangent), weight_second, NCOL, NROW)
    sigma = jax.nn.sigmoid(pre)
    delta = (back * sigma * (1.0 + pre * (1.0 - sigma))).astype(jnp.bfloat16)
    grad_first = kernel_grad(cube_pad, delta, NCOL, NROW)
    grad_second = kernel_grad(hidden_pad, cotangent, NCOL, NROW)
    return (features, grad_first, grad_second)
```

```python
import functools

import jax
import jax.numpy as jnp
from jax import lax
from jax.experimental import pallas as pl
from jax.experimental.pallas import tpu as pltpu
from jax.sharding import PartitionSpec as P

MESH = pl.DeviceIdType.MESH
VMEM_LIMIT = 56 * 1024 * 1024
BLOCK = 16


def build_shifts(x_ref, top_ref, bot_ref, shifts, pad):
    count, rows, chans = x_ref.shape
    if pad:
        zero = jnp.zeros((1, rows, chans), shifts.dtype)
        for q in range(3):
            shifts[q, 0:1] = zero
            shifts[q, count + 1 : count + 2] = zero
    step = 8 if count % 8 == 0 else 2
    row = lax.broadcasted_iota(jnp.int32, (step, rows, chans), 1)

    def one(i, carry):
        c = i * step
        x = x_ref[pl.ds(c, step)]
        shifts[1, pl.ds(c + pad, step)] = x
        wide = x.astype(jnp.float32)
        top = jnp.broadcast_to(top_ref[pl.ds(c, step)], wide.shape)
        bot = jnp.broadcast_to(bot_ref[pl.ds(c, step)], wide.shape)
        up = jnp.where(row == 0, top, pltpu.roll(wide, 1, 1))
        down = jnp.where(row == rows - 1, bot, pltpu.roll(wide, rows - 1, 1))
        shifts[0, pl.ds(c + pad, step)] = up.astype(shifts.dtype)
        shifts[2, pl.ds(c + pad, step)] = down.astype(shifts.dtype)
        return carry

    lax.fori_loop(0, count // step, one, 0)


def conv_kernel(pad, x_ref, top_ref, bot_ref, w_ref, out_ref, shifts):
    build_shifts(x_ref, top_ref, bot_ref, shifts, pad)
    rows, chans = x_ref.shape[1:]
    count = shifts.shape[1] - 2

    def one(i, carry):
        c = i * BLOCK
        total = None
        for q in range(3):
            for p in range(3):
                piece = shifts[q, pl.ds(c + p, BLOCK)].reshape(BLOCK * rows, chans)
                term = jnp.dot(piece, w_ref[p, q], preferred_element_type=jnp.float32)
                total = term if total is None else total + term
        out_ref[pl.ds(c * rows, BLOCK * rows)] = total.astype(out_ref.dtype)
        return carry

    lax.fori_loop(0, count // BLOCK, one, 0)


def conv(x, top, bot, w, pad, dtype):
    count = x.shape[0] - (0 if pad else 2)
    rows, chans = x.shape[1:]
    return pl.pallas_call(
        functools.partial(conv_kernel, pad),
        out_shape=jax.ShapeDtypeStruct((count * rows, w.shape[3]), dtype),
        in_specs=[pl.BlockSpec(memory_space=pltpu.VMEM)] * 4,
        out_specs=pl.BlockSpec(memory_space=pltpu.VMEM),
        scratch_shapes=[pltpu.VMEM((3, count + 2, rows, chans), jnp.bfloat16)],
        compiler_params=pltpu.CompilerParams(vmem_limit_bytes=VMEM_LIMIT),
        cost_estimate=pl.CostEstimate(
            flops=18 * count * rows * chans * w.shape[3],
            bytes_accessed=4 * x.size + 2 * w.size,
            transcendentals=0,
        ),
    )(x, top[:, None, :].astype(jnp.float32), bot[:, None, :].astype(jnp.float32), w)


def grad_kernel(pad, x_ref, top_ref, bot_ref, d_ref, out_ref, shifts, flipped, sums):
    build_shifts(x_ref, top_ref, bot_ref, shifts, pad)
    rows, chans = x_ref.shape[1:]
    count = shifts.shape[1] - 2
    cols = min(32, count)
    span = cols * rows

    def one(i, carry):
        c = i * cols
        for k in range(span // 256):
            block = d_ref[pl.ds(c * rows + k * 256, 256)]
            flipped[:, k * 256 : (k + 1) * 256] = block.T
        for q in range(3):
            for p in range(3):
                piece = shifts[q, pl.ds(c + p, cols)].reshape(span, chans)
                sums[p, q] += jnp.dot(flipped[...], piece, preferred_element_type=jnp.float32)
        return carry

    sums[...] = jnp.zeros_like(sums)
    lax.fori_loop(0, count // cols, one, 0)
    for p in range(3):
        for q in range(3):
            out_ref[p, q] = sums[p, q].T


def kernel_grad(x, top, bot, d, pad):
    count = x.shape[0] - (0 if pad else 2)
    rows, chans = x.shape[1:]
    outs = d.shape[1]
    return pl.pallas_call(
        functools.partial(grad_kernel, pad),
        out_shape=jax.ShapeDtypeStruct((3, 3, chans, outs), jnp.float32),
        in_specs=[pl.BlockSpec(memory_space=pltpu.VMEM)] * 4,
        out_specs=pl.BlockSpec(memory_space=pltpu.VMEM),
        scratch_shapes=[
            pltpu.VMEM((3, count + 2, rows, chans), jnp.bfloat16),
            pltpu.VMEM((outs, min(32, count) * rows), jnp.bfloat16),
            pltpu.VMEM((3, 3, outs, chans), jnp.float32),
        ],
        compiler_params=pltpu.CompilerParams(vmem_limit_bytes=VMEM_LIMIT),
        cost_estimate=pl.CostEstimate(
            flops=18 * count * rows * chans * outs,
            bytes_accessed=4 * x.size,
            transcendentals=0,
        ),
    )(x, top[:, None, :].astype(jnp.float32), bot[:, None, :].astype(jnp.float32), d)


def sum_kernel(axis, count, g_ref, out_ref, mine, landed, full, send, recv, send2, recv2):
    me = lax.axis_index(axis)
    chunk = g_ref.shape[0] // count
    barrier = pltpu.get_barrier_semaphore()
    for k in range(1, count):
        pl.semaphore_signal(
            barrier, inc=1, device_id={axis: lax.rem(me + k, count)}, device_id_type=MESH
        )
    mine[...] = g_ref[...].astype(mine.dtype)
    pl.semaphore_wait(barrier, count - 1)

    def rows_of(i):
        return pl.ds(pl.multiple_of(i * chunk, 16), chunk)

    def scatter(k):
        peer = lax.rem(me + k, count)
        return pltpu.make_async_remote_copy(
            src_ref=mine.at[rows_of(peer)],
            dst_ref=landed.at[k - 1],
            send_sem=send.at[k - 1],
            recv_sem=recv.at[k - 1],
            device_id={axis: peer},
            device_id_type=MESH,
        )

    def gather(k):
        return pltpu.make_async_remote_copy(
            src_ref=full.at[rows_of(me)],
            dst_ref=full.at[rows_of(me)],
            send_sem=send2.at[k - 1],
            recv_sem=recv2.at[k - 1],
            device_id={axis: lax.rem(me + k, count)},
            device_id_type=MESH,
        )

    first = [scatter(k) for k in range(1, count)]
    for copy in first:
        copy.start()
    total = g_ref[rows_of(me)]
    for k in range(1, count):
        first[k - 1].wait_recv()
        total = total + landed[k - 1].astype(jnp.float32)
    full[rows_of(me)] = total.astype(full.dtype)
    second = [gather(k) for k in range(1, count)]
    for copy in second:
        copy.start()
    out_ref[rows_of(me)] = full[rows_of(me)].astype(out_ref.dtype)
    for k in range(1, count):
        second[k - 1].wait_recv()
        source = rows_of(lax.rem(me + count - k, count))
        out_ref[source] = full[source].astype(out_ref.dtype)
    for copy in first + second:
        copy.wait_send()


def sum_over(g, axis):
    count = lax.axis_size(axis)
    given, cols = g.shape
    rows = -(-given // (16 * count)) * 16 * count
    if rows != given:
        g = jnp.pad(g, ((0, rows - given), (0, 0)))
    return pl.pallas_call(
        functools.partial(sum_kernel, axis, count),
        out_shape=jax.ShapeDtypeStruct((rows, cols), jnp.float32),
        in_specs=[pl.BlockSpec(memory_space=pltpu.VMEM)],
        out_specs=pl.BlockSpec(memory_space=pltpu.VMEM),
        scratch_shapes=[
            pltpu.VMEM((rows, cols), jnp.bfloat16),
            pltpu.VMEM((count - 1, rows // count, cols), jnp.bfloat16),
            pltpu.VMEM((rows, cols), jnp.bfloat16),
        ]
        + [pltpu.SemaphoreType.DMA((count - 1,))] * 4,
        compiler_params=pltpu.CompilerParams(
            collective_id=0, has_side_effects=True, vmem_limit_bytes=VMEM_LIMIT
        ),
        cost_estimate=pl.CostEstimate(flops=0, bytes_accessed=40 * g.size, transcendentals=0),
    )(g)[:given]


def neighbours(first, last, axis):
    count = lax.axis_size(axis)
    up = [(i, i + 1) for i in range(count - 1)]
    down = [(j, i) for i, j in up]
    return lax.ppermute(last, axis, up), lax.ppermute(first, axis, down)


def with_columns(x):
    before, after = neighbours(x[:1], x[-1:], "freq")
    return jnp.concatenate([before, x, after], axis=0)


def silu_slope(pre):
    sigma = jax.nn.sigmoid(pre)
    return sigma * (1.0 + pre * (1.0 - sigma))


def body(sky_cube, weight_first, weight_second, cotangent):
    strip, rows, chans = cotangent.shape
    top, bot = neighbours(sky_cube[:, 0], sky_cube[:, -1], "sky")
    partial = conv(sky_cube, top, bot, weight_first, 1, jnp.bfloat16)
    pre = lax.psum_scatter(partial, "freq", scatter_dimension=0, tiled=True)
    pre = pre.astype(jnp.float32)
    cot_pad = with_columns(cotangent)
    cot_top, cot_bot = neighbours(cot_pad[:, 0], cot_pad[:, -1], "sky")
    weight_back = jnp.transpose(weight_second[::-1, ::-1], (0, 1, 3, 2))
    back = conv(cot_pad, cot_top, cot_bot, weight_back, 0, jnp.float32)
    delta = (back * silu_slope(pre)).astype(jnp.bfloat16)
    whole = lax.all_gather(delta, "freq", axis=0, tiled=True)
    hidden = jax.nn.silu(pre).astype(jnp.bfloat16).reshape(strip, rows, chans)
    hidden_pad = with_columns(hidden)
    hid_top, hid_bot = neighbours(hidden_pad[:, 0], hidden_pad[:, -1], "sky")
    second = kernel_grad(hidden_pad, hid_top, hid_bot, cotangent.reshape(strip * rows, -1), 0)
    features = conv(hidden_pad, hid_top, hid_bot, weight_second, 0, jnp.bfloat16)
    grad_second = lax.psum(second.astype(jnp.bfloat16), ("freq", "sky")).astype(jnp.float32)
    first = kernel_grad(sky_cube, top, bot, whole, 1)
    grad_first = sum_over(first.reshape(-1, first.shape[3]), "sky").reshape(first.shape)
    return (features.reshape(strip, rows, -1), grad_first, grad_second)


def solution(mesh):
    return jax.shard_map(
        body,
        mesh=mesh,
        in_specs=(P(None, "sky", "freq"), P(None, None, "freq", None), P(), P("freq", "sky", None)),
        out_specs=(P("freq", "sky", None), P(None, None, "freq", None), P()),
        check_vma=False,
    )
```

```python
import functools

import jax
import jax.numpy as jnp
from jax import lax
from jax.experimental import pallas as pl
from jax.experimental.pallas import tpu as pltpu
from jax.sharding import PartitionSpec as P

MESH = pl.DeviceIdType.MESH
VMEM_LIMIT = 60 * 1024 * 1024
BLOCK = 16
F32 = jnp.float32
BF16 = jnp.bfloat16


def remote(src, dst, send, recv, axis, peer):
    return pltpu.make_async_remote_copy(
        src_ref=src,
        dst_ref=dst,
        send_sem=send,
        recv_sem=recv,
        device_id={axis: peer},
        device_id_type=MESH,
    )


def greet(targets):
    barrier = pltpu.get_barrier_semaphore()
    for axis, peer in targets:
        pl.semaphore_signal(barrier, inc=1, device_id={axis: peer}, device_id_type=MESH)
    pl.semaphore_wait(barrier, len(targets))


def take_edges(shifts, stage):
    rows = shifts.shape[2]

    def one(i, carry):
        c = pl.multiple_of(i * BLOCK, BLOCK)
        x = shifts[1, pl.ds(c, BLOCK)].astype(F32)
        stage[0, pl.ds(c, BLOCK)] = x[:, 0, :].astype(BF16)
        stage[1, pl.ds(c, BLOCK)] = x[:, rows - 1, :].astype(BF16)
        return carry

    lax.fori_loop(0, shifts.shape[1] // BLOCK, one, 0)


def row_copies(stage, halo, send, recv):
    sky = lax.axis_index("sky")
    down = remote(stage.at[0], halo.at[1], send.at[0], recv.at[1], "sky", sky - 1)
    up = remote(stage.at[1], halo.at[0], send.at[1], recv.at[0], "sky", sky + 1)
    return down, up


def send_rows(stage, halo, send, recv):
    sky, count = lax.axis_index("sky"), lax.axis_size("sky")
    down, up = row_copies(stage, halo, send, recv)

    @pl.when(sky > 0)
    def _():
        down.start()

    @pl.when(sky < count - 1)
    def _():
        up.start()

    @pl.when(sky == 0)
    def _():
        halo[0] = jnp.zeros(halo.shape[1:], halo.dtype)

    @pl.when(sky == count - 1)
    def _():
        halo[1] = jnp.zeros(halo.shape[1:], halo.dtype)


def land_rows(stage, halo, send, recv):
    sky, count = lax.axis_index("sky"), lax.axis_size("sky")
    down, up = row_copies(stage, halo, send, recv)

    @pl.when(sky > 0)
    def _():
        down.wait_send()
        up.wait_recv()

    @pl.when(sky < count - 1)
    def _():
        up.wait_send()
        down.wait_recv()


def column_copies(shifts, strip, send, recv):
    freq = lax.axis_index("freq")
    down = remote(shifts.at[1, 1], shifts.at[1, strip + 1], send.at[0], recv.at[1], "freq", freq - 1)
    up = remote(shifts.at[1, strip], shifts.at[1, 0], send.at[1], recv.at[0], "freq", freq + 1)
    return down, up


def send_columns(shifts, strip, send, recv):
    freq, count = lax.axis_index("freq"), lax.axis_size("freq")
    down, up = column_copies(shifts, strip, send, recv)
    line = jnp.zeros(shifts.shape[2:], shifts.dtype)

    @pl.when(freq > 0)
    def _():
        down.start()

    @pl.when(freq < count - 1)
    def _():
        up.start()

    @pl.when(freq == 0)
    def _():
        shifts[1, 0] = line

    @pl.when(freq == count - 1)
    def _():
        shifts[1, strip + 1] = line


def land_columns(shifts, strip, send, recv):
    freq, count = lax.axis_index("freq"), lax.axis_size("freq")
    down, up = column_copies(shifts, strip, send, recv)

    @pl.when(freq > 0)
    def _():
        down.wait_send()
        up.wait_recv()

    @pl.when(freq < count - 1)
    def _():
        up.wait_send()
        down.wait_recv()


def clear_tail(shifts, used):
    shifts[1, used:] = jnp.zeros((shifts.shape[1] - used,) + shifts.shape[2:], shifts.dtype)


def build_shifts(shifts, halo):
    rows, chans = shifts.shape[2:]
    step = BLOCK
    row = lax.broadcasted_iota(jnp.int32, (step, rows, chans), 1)

    def one(i, carry):
        c = pl.multiple_of(i * step, step)
        wide = shifts[1, pl.ds(c, step)].astype(F32)
        top = jnp.broadcast_to(halo[0, pl.ds(c, step)].astype(F32)[:, None, :], wide.shape)
        bot = jnp.broadcast_to(halo[1, pl.ds(c, step)].astype(F32)[:, None, :], wide.shape)
        up = jnp.where(row == 0, top, pltpu.roll(wide, 1, 1))
        down = jnp.where(row == rows - 1, bot, pltpu.roll(wide, rows - 1, 1))
        shifts[0, pl.ds(c, step)] = up.astype(BF16)
        shifts[2, pl.ds(c, step)] = down.astype(BF16)
        return carry

    lax.fori_loop(0, shifts.shape[1] // step, one, 0)


def conv_block(shifts, c, w_ref):
    rows, chans = shifts.shape[2:]
    total = None
    for q in range(3):
        for p in range(3):
            piece = shifts[q, pl.ds(c + p, BLOCK)].reshape(BLOCK * rows, chans)
            term = jnp.dot(piece, w_ref[p, q], preferred_element_type=F32)
            total = term if total is None else total + term
    return total


def add_grad(shifts, c, cols, d_ref, flipped, sums):
    rows, chans = shifts.shape[2:]
    span = cols * rows
    for k in range(span // 256):
        flipped[:, k * 256 : (k + 1) * 256] = d_ref[k * 256 : (k + 1) * 256].T
    for q in range(3):
        for p in range(3):
            piece = shifts[q, pl.ds(c + p, cols)].reshape(span, chans)
            sums[p, q] += jnp.dot(flipped[...], piece, preferred_element_type=F32)


def main_kernel(
    x_hbm, w1_ref, w2_ref, w2b_ref, cot_ref,
    feat_ref, g1_ref, g2_ref,
    xs, cs, hs, xstage, xhalo, cstage, chalo, hstage, hhalo,
    give, got, part, mid, landed, own, back, dall, flipped,
    load_sem, row_send, row_recv, col_send, col_recv,
    give_send, give_recv, mid_send, mid_recv,
    far_send, far_recv, near_send, near_recv, pass_send, pass_recv,
):
    freq, nf = lax.axis_index("freq"), lax.axis_size("freq")
    sky, ns = lax.axis_index("sky"), lax.axis_size("sky")
    ny = nf // 2
    y, core = freq // 2, freq % 2
    partner = y * 2 + 1 - core
    count, rows = x_hbm.shape[:2]
    strip = count // nf
    blocks = strip // BLOCK
    size = BLOCK * rows

    load = pltpu.make_async_copy(x_hbm, xs.at[1, pl.ds(1, count)], load_sem)
    load.start()
    xs[1, 0] = jnp.zeros(xs.shape[2:], BF16)
    clear_tail(xs, count + 1)
    clear_tail(cs, strip + 2)
    clear_tail(hs, strip + 2)
    cs[1, 1 : strip + 1] = cot_ref[...]
    greet(
        [("freq", lax.rem(freq + k, nf)) for k in range(1, nf)]
        + [("sky", lax.rem(sky + 1, ns)), ("sky", lax.rem(sky + ns - 1, ns))]
    )
    send_columns(cs, strip, col_send.at[0], col_recv.at[0])
    load.wait()
    take_edges(xs, xstage)
    send_rows(xstage, xhalo, row_send.at[0], row_recv.at[0])
    land_columns(cs, strip, col_send.at[0], col_recv.at[0])
    take_edges(cs, cstage)
    send_rows(cstage, chalo, row_send.at[1], row_recv.at[1])
    land_rows(xstage, xhalo, row_send.at[0], row_recv.at[0])
    build_shifts(xs, xhalo)

    def give_copy(t):
        return remote(
            give.at[t], got.at[t], give_send.at[t], give_recv.at[t], "freq", partner
        )

    def mid_copy(t):
        peer = lax.rem(y + 1 + t // blocks, ny) * 2 + core
        return remote(mid.at[t], landed.at[t], mid_send.at[t], mid_recv.at[t], "freq", peer)

    away = (ny - 1) * blocks
    steps = ny * blocks

    def one(t, carry):
        @pl.when(t < steps)
        def _():
            dest = lax.rem(y + 1 + t // blocks, ny) * 2
            sub = lax.rem(t, blocks) * BLOCK
            give[t] = conv_block(xs, (dest + 1 - core) * strip + sub, w1_ref).astype(BF16)
            give_copy(t).start()
            part[lax.rem(t, 2)] = conv_block(xs, (dest + core) * strip + sub, w1_ref)

        @pl.when(t > 0)
        def _():
            before = t - 1
            give_copy(before).wait_recv()
            total = part[lax.rem(before, 2)] + got[before].astype(F32)

            @pl.when(before < away)
            def _():
                mid[before] = total.astype(BF16)
                mid_copy(before).start()

            @pl.when(before >= away)
            def _():
                own[before - away] = total

        return carry

    lax.fori_loop(0, steps + 1, one, 0)

    land_rows(cstage, chalo, row_send.at[1], row_recv.at[1])
    build_shifts(cs, chalo)

    def one_back(i, carry):
        back[i] = conv_block(cs, i * BLOCK, w2b_ref)
        return carry

    lax.fori_loop(0, blocks, one_back, 0)

    def one_pre(i, carry):
        pre = own[i]
        for dy in range(ny - 1):
            mid_copy(dy * blocks + i).wait_recv()
            pre = pre + landed[dy * blocks + i].astype(F32)
        sigma = jax.nn.sigmoid(pre)
        hs[1, pl.ds(1 + i * BLOCK, BLOCK)] = (pre * sigma).astype(BF16).reshape(BLOCK, rows, -1)
        delta = back[i] * sigma * (1.0 + pre * (1.0 - sigma))
        dall[freq, pl.ds(pl.multiple_of(i * size, size), size)] = delta.astype(BF16)
        return carry

    lax.fori_loop(0, blocks, one_pre, 0)

    send_columns(hs, strip, col_send.at[1], col_recv.at[1])

    def far_copy(dy):
        peer = lax.rem(y + dy, ny) * 2 + core
        return remote(
            dall.at[freq], dall.at[freq], far_send.at[dy - 1], far_recv.at[dy - 1], "freq", peer
        )

    def pass_copy(dy):
        owner = lax.rem(y + ny - dy, ny) * 2 + core
        return remote(
            dall.at[owner], dall.at[owner], pass_send.at[dy - 1], pass_recv.at[dy - 1],
            "freq", partner,
        )

    near = remote(dall.at[freq], dall.at[freq], near_send, near_recv, "freq", partner)
    for dy in range(1, ny):
        far_copy(dy).start()
    near.start()
    land_columns(hs, strip, col_send.at[1], col_recv.at[1])
    take_edges(hs, hstage)
    send_rows(hstage, hhalo, row_send.at[2], row_recv.at[2])

    g1_ref[...] = jnp.zeros_like(g1_ref)
    g2_ref[...] = jnp.zeros_like(g2_ref)
    add_grad(xs, freq * strip, strip, dall.at[freq], flipped, g1_ref)
    land_rows(hstage, hhalo, row_send.at[2], row_recv.at[2])
    build_shifts(hs, hhalo)

    def one_feature(i, carry):
        value = conv_block(hs, i * BLOCK, w2_ref)
        feat_ref[pl.ds(pl.multiple_of(i * size, size), size)] = value.astype(feat_ref.dtype)
        return carry

    lax.fori_loop(0, blocks, one_feature, 0)
    near.wait_recv()
    add_grad(xs, partner * strip, strip, dall.at[partner], flipped, g1_ref)
    add_grad(hs, 0, strip, cot_ref.reshape(strip * rows, -1), flipped, g2_ref)
    for dy in range(1, ny):
        far_copy(dy).wait_recv()
        pass_copy(dy).start()
        owner = lax.rem(y + ny - dy, ny) * 2
        add_grad(xs, (owner + core) * strip, strip, dall.at[owner + core], flipped, g1_ref)
    for dy in range(1, ny):
        pass_copy(dy).wait_recv()
        owner = lax.rem(y + ny - dy, ny) * 2
        add_grad(xs, (owner + 1 - core) * strip, strip, dall.at[owner + 1 - core], flipped, g1_ref)

    def drain(t, carry):
        give_copy(t).wait_send()

        @pl.when(t < away)
        def _():
            mid_copy(t).wait_send()

        return carry

    lax.fori_loop(0, steps, drain, 0)
    near.wait_send()
    for dy in range(1, ny):
        far_copy(dy).wait_send()
        pass_copy(dy).wait_send()


def main_call(x, w1, w2, w2b, cot):
    nf = lax.axis_size("freq")
    ny = nf // 2
    count, rows, chans = x.shape
    strip, _, outs = cot.shape
    hid = w1.shape[3]
    blocks = strip // BLOCK
    size = BLOCK * rows
    steps, away = ny * blocks, (ny - 1) * blocks
    wide, thin = count + BLOCK, strip + BLOCK
    vmem = pl.BlockSpec(memory_space=pltpu.VMEM)
    dma = pltpu.SemaphoreType.DMA
    return pl.pallas_call(
        main_kernel,
        out_shape=(
            jax.ShapeDtypeStruct((strip * rows, outs), BF16),
            jax.ShapeDtypeStruct((3, 3, hid, chans), F32),
            jax.ShapeDtypeStruct((3, 3, outs, hid), F32),
        ),
        in_specs=[pl.BlockSpec(memory_space=pl.ANY)] + [vmem] * 4,
        out_specs=(vmem,) * 3,
        scratch_shapes=[
            pltpu.VMEM((3, wide, rows, chans), BF16),
            pltpu.VMEM((3, thin, rows, outs), BF16),
            pltpu.VMEM((3, thin, rows, hid), BF16),
            pltpu.VMEM((2, wide, chans), BF16),
            pltpu.VMEM((2, wide, chans), BF16),
            pltpu.VMEM((2, thin, outs), BF16),
            pltpu.VMEM((2, thin, outs), BF16),
            pltpu.VMEM((2, thin, hid), BF16),
            pltpu.VMEM((2, thin, hid), BF16),
            pltpu.VMEM((steps, size, hid), BF16),
            pltpu.VMEM((steps, size, hid), BF16),
            pltpu.VMEM((2, size, hid), F32),
            pltpu.VMEM((away, size, hid), BF16),
            pltpu.VMEM((away, size, hid), BF16),
            pltpu.VMEM((blocks, size, hid), F32),
            pltpu.VMEM((blocks, size, hid), F32),
            pltpu.VMEM((nf, strip * rows, hid), BF16),
            pltpu.VMEM((hid, strip * rows), BF16),
            dma,
            dma((3, 2)), dma((3, 2)), dma((2, 2)), dma((2, 2)),
            dma((steps,)), dma((steps,)), dma((away,)), dma((away,)),
            dma((ny - 1,)), dma((ny - 1,)), dma, dma, dma((ny - 1,)), dma((ny - 1,)),
        ],
        compiler_params=pltpu.CompilerParams(
            collective_id=1, has_side_effects=True, vmem_limit_bytes=VMEM_LIMIT
        ),
        cost_estimate=pl.CostEstimate(
            flops=36 * count * rows * chans * hid, bytes_accessed=4 * x.size, transcendentals=0
        ),
    )(x, w1, w2, w2b, cot)


def sum_kernel(
    g1_ref, g2_ref, o1_ref, o2_ref,
    mine1, landed1, full1, mine2, landed2, share, landed3, full3, full4, full2,
    s1, r1, s2, r2, s3, r3, s4, r4, s5, r5, s6, r6,
):
    freq, nf = lax.axis_index("freq"), lax.axis_size("freq")
    sky, ns = lax.axis_index("sky"), lax.axis_size("sky")
    chunk1 = g1_ref.shape[0] // ns
    chunk2 = g2_ref.shape[0] // nf
    chunk3 = share.shape[0] // ns

    def rows_of(i, chunk):
        return pl.ds(pl.multiple_of(i * chunk, 16), chunk)

    def scatter(axis, me, n, src, dst, chunk, send, recv):
        out = []
        for k in range(1, n):
            peer = lax.rem(me + k, n)
            out.append(
                remote(src.at[rows_of(peer, chunk)], dst.at[k - 1], send.at[k - 1],
                       recv.at[k - 1], axis, peer)
            )
        return out

    def gather(axis, me, n, full, chunk, send, recv):
        here = full.at[rows_of(me, chunk)]
        return [
            remote(here, here, send.at[k - 1], recv.at[k - 1], axis, lax.rem(me + k, n))
            for k in range(1, n)
        ]

    def start(copies):
        for copy in copies:
            copy.start()

    def collect(copies, landed, total):
        for k, copy in enumerate(copies):
            copy.wait_recv()
            total = total + landed[k].astype(F32)
        return total

    mine1[...] = g1_ref[...].astype(BF16)
    mine2[...] = g2_ref[...].astype(BF16)
    share[chunk2:] = jnp.zeros((share.shape[0] - chunk2, share.shape[1]), F32)
    greet(
        [("freq", lax.rem(freq + k, nf)) for k in range(1, nf)]
        + [("sky", lax.rem(sky + k, ns)) for k in range(1, ns)]
    )
    a2 = scatter("freq", freq, nf, mine2, landed2, chunk2, s2, r2)
    start(a2)
    a1 = scatter("sky", sky, ns, mine1, landed1, chunk1, s1, r1)
    start(a1)
    share[:chunk2] = collect(a2, landed2, g2_ref[rows_of(freq, chunk2)])
    full3[...] = share[...].astype(BF16)
    a3 = scatter("sky", sky, ns, full3, landed3, chunk3, s3, r3)
    start(a3)
    full1[rows_of(sky, chunk1)] = collect(a1, landed1, g1_ref[rows_of(sky, chunk1)]).astype(BF16)
    b1 = gather("sky", sky, ns, full1, chunk1, s4, r4)
    start(b1)
    total3 = collect(a3, landed3, share[rows_of(sky, chunk3)])
    full4[rows_of(sky, chunk3)] = total3.astype(BF16)
    b3 = gather("sky", sky, ns, full4, chunk3, s5, r5)
    start(b3)
    for copy in b3:
        copy.wait_recv()
    full2[rows_of(freq, chunk2)] = full4[:chunk2]
    b2 = gather("freq", freq, nf, full2, chunk2, s6, r6)
    start(b2)
    for copy in b1:
        copy.wait_recv()
    o1_ref[...] = full1[...].astype(F32)
    for copy in b2:
        copy.wait_recv()
    o2_ref[...] = full2[...].astype(F32)
    for copy in a1 + a2 + a3 + b1 + b2 + b3:
        copy.wait_send()


def sum_call(g1, g2):
    nf, ns = lax.axis_size("freq"), lax.axis_size("sky")
    rows1, cols1 = g1.shape
    rows2, cols2 = g2.shape
    chunk1, chunk2 = rows1 // ns, rows2 // nf
    chunk3 = -(-chunk2 // (16 * ns)) * 16
    vmem = pl.BlockSpec(memory_space=pltpu.VMEM)
    dma = pltpu.SemaphoreType.DMA
    along = [dma((ns - 1,))] * 2
    across = [dma((nf - 1,))] * 2
    return pl.pallas_call(
        sum_kernel,
        out_shape=(
            jax.ShapeDtypeStruct((rows1, cols1), F32),
            jax.ShapeDtypeStruct((rows2, cols2), F32),
        ),
        in_specs=[vmem] * 2,
        out_specs=(vmem,) * 2,
        scratch_shapes=[
            pltpu.VMEM((rows1, cols1), BF16),
            pltpu.VMEM((ns - 1, chunk1, cols1), BF16),
            pltpu.VMEM((rows1, cols1), BF16),
            pltpu.VMEM((rows2, cols2), BF16),
            pltpu.VMEM((nf - 1, chunk2, cols2), BF16),
            pltpu.VMEM((ns * chunk3, cols2), F32),
            pltpu.VMEM((ns - 1, chunk3, cols2), BF16),
            pltpu.VMEM((ns * chunk3, cols2), BF16),
            pltpu.VMEM((ns * chunk3, cols2), BF16),
            pltpu.VMEM((rows2, cols2), BF16),
        ]
        + along + across + along + along + along + across,
        compiler_params=pltpu.CompilerParams(
            collective_id=0, has_side_effects=True, vmem_limit_bytes=VMEM_LIMIT
        ),
        cost_estimate=pl.CostEstimate(flops=0, bytes_accessed=40 * g1.size, transcendentals=0),
    )(g1, g2)


def body(sky_cube, weight_first, weight_second, cotangent):
    strip, rows, _ = cotangent.shape
    weight_back = jnp.transpose(weight_second[::-1, ::-1], (0, 1, 3, 2))
    features, first, second = main_call(
        sky_cube, weight_first, weight_second, weight_back, cotangent
    )
    sum_first, sum_second = sum_call(
        first.reshape(-1, first.shape[3]), second.reshape(-1, second.shape[3])
    )
    grad_first = jnp.transpose(sum_first.reshape(first.shape), (0, 1, 3, 2))
    grad_second = jnp.transpose(sum_second.reshape(second.shape), (0, 1, 3, 2))
    return (features.reshape(strip, rows, -1), grad_first, grad_second)


def solution(mesh):
    return jax.shard_map(
        body,
        mesh=mesh,
        in_specs=(P(None, "sky", "freq"), P(None, None, "freq", None), P(), P("freq", "sky", None)),
        out_specs=(P("freq", "sky", None), P(None, None, "freq", None), P()),
        check_vma=False,
    )
```

```python
import functools

import jax
import jax.numpy as jnp
from jax import lax
from jax.experimental import pallas as pl
from jax.experimental.pallas import tpu as pltpu
from jax.sharding import PartitionSpec as P

MESH = pl.DeviceIdType.MESH
VMEM_LIMIT = 60 * 1024 * 1024
BLOCK = 16
F32 = jnp.float32
BF16 = jnp.bfloat16


def remote(src, dst, send, recv, axis, peer):
    return pltpu.make_async_remote_copy(
        src_ref=src,
        dst_ref=dst,
        send_sem=send,
        recv_sem=recv,
        device_id={axis: peer},
        device_id_type=MESH,
    )


def greet(targets):
    barrier = pltpu.get_barrier_semaphore()
    for axis, peer in targets:
        pl.semaphore_signal(barrier, inc=1, device_id={axis: peer}, device_id_type=MESH)
    pl.semaphore_wait(barrier, len(targets))


def take_edges(shifts, stage):
    rows = shifts.shape[2]

    def one(i, carry):
        c = pl.multiple_of(i * BLOCK, BLOCK)
        x = shifts[1, pl.ds(c, BLOCK)].astype(F32)
        stage[0, pl.ds(c, BLOCK)] = x[:, 0, :].astype(BF16)
        stage[1, pl.ds(c, BLOCK)] = x[:, rows - 1, :].astype(BF16)
        return carry

    lax.fori_loop(0, shifts.shape[1] // BLOCK, one, 0)


def row_copies(stage, halo, send, recv):
    sky = lax.axis_index("sky")
    down = remote(stage.at[0], halo.at[1], send.at[0], recv.at[1], "sky", sky - 1)
    up = remote(stage.at[1], halo.at[0], send.at[1], recv.at[0], "sky", sky + 1)
    return down, up


def send_rows(stage, halo, send, recv):
    sky, count = lax.axis_index("sky"), lax.axis_size("sky")
    down, up = row_copies(stage, halo, send, recv)

    @pl.when(sky > 0)
    def _():
        down.start()

    @pl.when(sky < count - 1)
    def _():
        up.start()

    @pl.when(sky == 0)
    def _():
        halo[0] = jnp.zeros(halo.shape[1:], halo.dtype)

    @pl.when(sky == count - 1)
    def _():
        halo[1] = jnp.zeros(halo.shape[1:], halo.dtype)


def land_rows(stage, halo, send, recv):
    sky, count = lax.axis_index("sky"), lax.axis_size("sky")
    down, up = row_copies(stage, halo, send, recv)

    @pl.when(sky > 0)
    def _():
        down.wait_send()
        up.wait_recv()

    @pl.when(sky < count - 1)
    def _():
        up.wait_send()
        down.wait_recv()


def column_copies(shifts, strip, send, recv):
    freq = lax.axis_index("freq")
    down = remote(shifts.at[1, 1], shifts.at[1, strip + 1], send.at[0], recv.at[1], "freq", freq - 1)
    up = remote(shifts.at[1, strip], shifts.at[1, 0], send.at[1], recv.at[0], "freq", freq + 1)
    return down, up


def send_columns(shifts, strip, send, recv):
    freq, count = lax.axis_index("freq"), lax.axis_size("freq")
    down, up = column_copies(shifts, strip, send, recv)
    line = jnp.zeros(shifts.shape[2:], shifts.dtype)

    @pl.when(freq > 0)
    def _():
        down.start()

    @pl.when(freq < count - 1)
    def _():
        up.start()

    @pl.when(freq == 0)
    def _():
        shifts[1, 0] = line

    @pl.when(freq == count - 1)
    def _():
        shifts[1, strip + 1] = line


def land_columns(shifts, strip, send, recv):
    freq, count = lax.axis_index("freq"), lax.axis_size("freq")
    down, up = column_copies(shifts, strip, send, recv)

    @pl.when(freq > 0)
    def _():
        down.wait_send()
        up.wait_recv()

    @pl.when(freq < count - 1)
    def _():
        up.wait_send()
        down.wait_recv()


def clear_tail(shifts, used):
    shifts[1, used:] = jnp.zeros((shifts.shape[1] - used,) + shifts.shape[2:], shifts.dtype)


def build_shifts(shifts, halo):
    rows, chans = shifts.shape[2:]
    step = BLOCK
    row = lax.broadcasted_iota(jnp.int32, (step, rows, chans), 1)

    def one(i, carry):
        c = pl.multiple_of(i * step, step)
        wide = shifts[1, pl.ds(c, step)].astype(F32)
        top = jnp.broadcast_to(halo[0, pl.ds(c, step)].astype(F32)[:, None, :], wide.shape)
        bot = jnp.broadcast_to(halo[1, pl.ds(c, step)].astype(F32)[:, None, :], wide.shape)
        up = jnp.where(row == 0, top, pltpu.roll(wide, 1, 1))
        down = jnp.where(row == rows - 1, bot, pltpu.roll(wide, rows - 1, 1))
        shifts[0, pl.ds(c, step)] = up.astype(BF16)
        shifts[2, pl.ds(c, step)] = down.astype(BF16)
        return carry

    lax.fori_loop(0, shifts.shape[1] // step, one, 0)


def conv_block(shifts, c, w_ref):
    rows, chans = shifts.shape[2:]
    pieces = [
        shifts[q, pl.ds(c + p, BLOCK)].reshape(BLOCK * rows, chans)
        for p in range(3)
        for q in range(3)
    ]
    return jnp.dot(
        jnp.concatenate(pieces, axis=1),
        w_ref[...].reshape(9 * chans, -1),
        preferred_element_type=F32,
    )


def add_grad(shifts, c, cols, d_ref, flipped, sums):
    rows, chans = shifts.shape[2:]
    span = cols * rows
    for k in range(span // 256):
        flipped[:, k * 256 : (k + 1) * 256] = d_ref[k * 256 : (k + 1) * 256].T
    for q in range(3):
        for p in range(3):
            piece = shifts[q, pl.ds(c + p, cols)].reshape(span, chans)
            sums[p, q] += jnp.dot(flipped[...], piece, preferred_element_type=F32)


def main_kernel(
    x_hbm, w1_ref, w2_ref, w2b_ref, cot_ref,
    feat_ref, g1_ref, g2_ref,
    xs, cs, hs, xstage, xhalo, cstage, chalo, hstage, hhalo,
    give, got, part, mid, landed, own, back, dall, flipped,
    load_sem, row_send, row_recv, col_send, col_recv,
    give_send, give_recv, mid_send, mid_recv,
    far_send, far_recv, near_send, near_recv, pass_send, pass_recv,
):
    freq, nf = lax.axis_index("freq"), lax.axis_size("freq")
    sky, ns = lax.axis_index("sky"), lax.axis_size("sky")
    ny = nf // 2
    y, core = freq // 2, freq % 2
    partner = y * 2 + 1 - core
    count, rows = x_hbm.shape[:2]
    strip = count // nf
    blocks = strip // BLOCK
    size = BLOCK * rows

    load = pltpu.make_async_copy(x_hbm, xs.at[1, pl.ds(1, count)], load_sem)
    load.start()
    xs[1, 0] = jnp.zeros(xs.shape[2:], BF16)
    clear_tail(xs, count + 1)
    clear_tail(cs, strip + 2)
    clear_tail(hs, strip + 2)
    cs[1, 1 : strip + 1] = cot_ref[...]
    greet(
        [("freq", lax.rem(freq + k, nf)) for k in range(1, nf)]
        + [("sky", lax.rem(sky + 1, ns)), ("sky", lax.rem(sky + ns - 1, ns))]
    )
    send_columns(cs, strip, col_send.at[0], col_recv.at[0])
    load.wait()
    take_edges(xs, xstage)
    send_rows(xstage, xhalo, row_send.at[0], row_recv.at[0])
    land_columns(cs, strip, col_send.at[0], col_recv.at[0])
    take_edges(cs, cstage)
    send_rows(cstage, chalo, row_send.at[1], row_recv.at[1])
    land_rows(xstage, xhalo, row_send.at[0], row_recv.at[0])
    build_shifts(xs, xhalo)

    def give_copy(t):
        return remote(
            give.at[t], got.at[t], give_send.at[t], give_recv.at[t], "freq", partner
        )

    def mid_copy(t):
        peer = lax.rem(y + 1 + t // blocks, ny) * 2 + core
        return remote(mid.at[t], landed.at[t], mid_send.at[t], mid_recv.at[t], "freq", peer)

    away = (ny - 1) * blocks
    steps = ny * blocks

    def one(t, carry):
        @pl.when(t < steps)
        def _():
            dest = lax.rem(y + 1 + t // blocks, ny) * 2
            sub = lax.rem(t, blocks) * BLOCK
            give[t] = conv_block(xs, (dest + 1 - core) * strip + sub, w1_ref).astype(BF16)
            give_copy(t).start()
            part[lax.rem(t, 2)] = conv_block(xs, (dest + core) * strip + sub, w1_ref)

        @pl.when(t > 0)
        def _():
            before = t - 1
            give_copy(before).wait_recv()
            total = part[lax.rem(before, 2)] + got[before].astype(F32)

            @pl.when(before < away)
            def _():
                mid[before] = total.astype(BF16)
                mid_copy(before).start()

            @pl.when(before >= away)
            def _():
                own[before - away] = total

        return carry

    lax.fori_loop(0, steps + 1, one, 0)

    land_rows(cstage, chalo, row_send.at[1], row_recv.at[1])
    build_shifts(cs, chalo)

    def one_back(i, carry):
        back[i] = conv_block(cs, i * BLOCK, w2b_ref)
        return carry

    lax.fori_loop(0, blocks, one_back, 0)

    def one_pre(i, carry):
        pre = own[i]
        for dy in range(ny - 1):
            mid_copy(dy * blocks + i).wait_recv()
            pre = pre + landed[dy * blocks + i].astype(F32)
        sigma = jax.nn.sigmoid(pre)
        hs[1, pl.ds(1 + i * BLOCK, BLOCK)] = (pre * sigma).astype(BF16).reshape(BLOCK, rows, -1)
        delta = back[i] * sigma * (1.0 + pre * (1.0 - sigma))
        dall[freq, pl.ds(pl.multiple_of(i * size, size), size)] = delta.astype(BF16)
        return carry

    lax.fori_loop(0, blocks, one_pre, 0)

    send_columns(hs, strip, col_send.at[1], col_recv.at[1])

    def far_copy(dy):
        peer = lax.rem(y + dy, ny) * 2 + core
        return remote(
            dall.at[freq], dall.at[freq], far_send.at[dy - 1], far_recv.at[dy - 1], "freq", peer
        )

    def pass_copy(dy):
        owner = lax.rem(y + ny - dy, ny) * 2 + core
        return remote(
            dall.at[owner], dall.at[owner], pass_send.at[dy - 1], pass_recv.at[dy - 1],
            "freq", partner,
        )

    near = remote(dall.at[freq], dall.at[freq], near_send, near_recv, "freq", partner)
    for dy in range(1, ny):
        far_copy(dy).start()
    near.start()
    land_columns(hs, strip, col_send.at[1], col_recv.at[1])
    take_edges(hs, hstage)
    send_rows(hstage, hhalo, row_send.at[2], row_recv.at[2])

    g1_ref[...] = jnp.zeros_like(g1_ref)
    g2_ref[...] = jnp.zeros_like(g2_ref)
    add_grad(xs, freq * strip, strip, dall.at[freq], flipped, g1_ref)
    land_rows(hstage, hhalo, row_send.at[2], row_recv.at[2])
    build_shifts(hs, hhalo)

    def one_feature(i, carry):
        value = conv_block(hs, i * BLOCK, w2_ref)
        feat_ref[pl.ds(pl.multiple_of(i * size, size), size)] = value.astype(feat_ref.dtype)
        return carry

    lax.fori_loop(0, blocks, one_feature, 0)
    near.wait_recv()
    add_grad(xs, partner * strip, strip, dall.at[partner], flipped, g1_ref)
    add_grad(hs, 0, strip, cot_ref.reshape(strip * rows, -1), flipped, g2_ref)
    for dy in range(1, ny):
        far_copy(dy).wait_recv()
        pass_copy(dy).start()
        owner = lax.rem(y + ny - dy, ny) * 2
        add_grad(xs, (owner + core) * strip, strip, dall.at[owner + core], flipped, g1_ref)
    for dy in range(1, ny):
        pass_copy(dy).wait_recv()
        owner = lax.rem(y + ny - dy, ny) * 2
        add_grad(xs, (owner + 1 - core) * strip, strip, dall.at[owner + 1 - core], flipped, g1_ref)

    def drain(t, carry):
        give_copy(t).wait_send()

        @pl.when(t < away)
        def _():
            mid_copy(t).wait_send()

        return carry

    lax.fori_loop(0, steps, drain, 0)
    near.wait_send()
    for dy in range(1, ny):
        far_copy(dy).wait_send()
        pass_copy(dy).wait_send()


def main_call(x, w1, w2, w2b, cot):
    nf = lax.axis_size("freq")
    ny = nf // 2
    count, rows, chans = x.shape
    strip, _, outs = cot.shape
    hid = w1.shape[3]
    blocks = strip // BLOCK
    size = BLOCK * rows
    steps, away = ny * blocks, (ny - 1) * blocks
    wide, thin = count + BLOCK, strip + BLOCK
    vmem = pl.BlockSpec(memory_space=pltpu.VMEM)
    dma = pltpu.SemaphoreType.DMA
    return pl.pallas_call(
        main_kernel,
        out_shape=(
            jax.ShapeDtypeStruct((strip * rows, outs), BF16),
            jax.ShapeDtypeStruct((3, 3, hid, chans), F32),
            jax.ShapeDtypeStruct((3, 3, outs, hid), F32),
        ),
        in_specs=[pl.BlockSpec(memory_space=pl.ANY)] + [vmem] * 4,
        out_specs=(vmem,) * 3,
        scratch_shapes=[
            pltpu.VMEM((3, wide, rows, chans), BF16),
            pltpu.VMEM((3, thin, rows, outs), BF16),
            pltpu.VMEM((3, thin, rows, hid), BF16),
            pltpu.VMEM((2, wide, chans), BF16),
            pltpu.VMEM((2, wide, chans), BF16),
            pltpu.VMEM((2, thin, outs), BF16),
            pltpu.VMEM((2, thin, outs), BF16),
            pltpu.VMEM((2, thin, hid), BF16),
            pltpu.VMEM((2, thin, hid), BF16),
            pltpu.VMEM((steps, size, hid), BF16),
            pltpu.VMEM((steps, size, hid), BF16),
            pltpu.VMEM((2, size, hid), F32),
            pltpu.VMEM((away, size, hid), BF16),
            pltpu.VMEM((away, size, hid), BF16),
            pltpu.VMEM((blocks, size, hid), F32),
            pltpu.VMEM((blocks, size, hid), F32),
            pltpu.VMEM((nf, strip * rows, hid), BF16),
            pltpu.VMEM((hid, strip * rows), BF16),
            dma,
            dma((3, 2)), dma((3, 2)), dma((2, 2)), dma((2, 2)),
            dma((steps,)), dma((steps,)), dma((away,)), dma((away,)),
            dma((ny - 1,)), dma((ny - 1,)), dma, dma, dma((ny - 1,)), dma((ny - 1,)),
        ],
        compiler_params=pltpu.CompilerParams(
            collective_id=1, has_side_effects=True, vmem_limit_bytes=VMEM_LIMIT
        ),
        cost_estimate=pl.CostEstimate(
            flops=36 * count * rows * chans * hid, bytes_accessed=4 * x.size, transcendentals=0
        ),
    )(x, w1, w2, w2b, cot)


def sum_kernel(pieces, nx, g1_ref, g2_ref, o1_ref, o2_ref, *refs):
    refs = list(refs)
    freq, nf = lax.axis_index("freq"), lax.axis_size("freq")
    sky, ns = lax.axis_index("sky"), lax.axis_size("sky")
    ny, nz = nf // 2, ns // nx
    y, core = freq // 2, freq % 2
    z, x = sky // nx, sky % nx
    partner = y * 2 + 1 - core
    half = g2_ref.shape[0] // 2
    chunk = half // ny
    side, side_in, mine2, side_y, landed2, joined, full2 = refs[:7]
    core_sems, y_sems, x_sems, z_sems = refs[7:11]
    rest = refs[11:]
    sets = [rest[6 * i : 6 * i + 6] for i in range(len(pieces))]

    def rows_of(i, size):
        return pl.ds(pl.multiple_of(i * size, 16), size)

    def start(copies):
        for copy in copies:
            copy.start()
        return copies

    def land(copies):
        for copy in copies:
            copy.wait_recv()

    def x_peer(k):
        return z * nx + lax.rem(x + k, nx)

    def z_peer(k):
        return lax.rem(z + k, nz) * nx + x

    def y_peer(k):
        return lax.rem(y + k, ny)

    greet(
        [("freq", partner)]
        + [("freq", y_peer(k) * 2 + core) for k in range(1, ny)]
        + [("sky", x_peer(k)) for k in range(1, nx)]
        + [("sky", z_peer(k)) for k in range(1, nz)]
    )
    done = []
    side[...] = g2_ref[rows_of(1 - core, half)].astype(BF16)
    core_out = remote(side, side_in, core_sems.at[0, 0], core_sems.at[0, 1], "freq", partner)
    done += start([core_out])

    def x_scatter(i):
        src, land_x = sets[i][0], sets[i][1]
        size = pieces[i][1] // nx
        return start([
            remote(src.at[rows_of(lax.rem(x + k, nx), size)], land_x.at[k - 1],
                   x_sems.at[0, i, k - 1], x_sems.at[1, i, k - 1], "sky", x_peer(k))
            for k in range(1, nx)
        ])

    def z_scatter(i):
        mid, land_z = sets[i][3], sets[i][4]
        size = pieces[i][1] // ns
        return start([
            remote(mid.at[rows_of(lax.rem(z + k, nz), size)], land_z.at[k - 1],
                   z_sems.at[0, i, k - 1], z_sems.at[1, i, k - 1], "sky", z_peer(k))
            for k in range(1, nz)
        ])

    def z_gather(i):
        size = pieces[i][1] // ns
        here = sets[i][5].at[rows_of(x * nz + z, size)]
        return start([
            remote(here, here, z_sems.at[2, i, k - 1], z_sems.at[3, i, k - 1], "sky", z_peer(k))
            for k in range(1, nz)
        ])

    def x_gather(i):
        size = pieces[i][1] // nx
        here = sets[i][5].at[rows_of(x, size)]
        return start([
            remote(here, here, x_sems.at[2, i, k - 1], x_sems.at[3, i, k - 1], "sky", x_peer(k))
            for k in range(1, nx)
        ])

    count = len(pieces)
    flights = {}
    for i in range(count - 1):
        first, size = pieces[i]
        sets[i][0][...] = g1_ref[first : first + size].astype(BF16)
        flights[i] = x_scatter(i)

    core_out.wait_recv()
    mine2[...] = g2_ref[rows_of(core, half)] + side_in[...].astype(F32)
    side_y[...] = mine2[...].astype(BF16)
    y_out = start([
        remote(side_y.at[rows_of(y_peer(k), chunk)],
               landed2.at[k - 1], y_sems.at[0, k - 1], y_sems.at[1, k - 1],
               "freq", y_peer(k) * 2 + core)
        for k in range(1, ny)
    ])

    def x_sum(i, own):
        size = pieces[i][1] // nx
        land(flights[i])
        done.extend(flights[i])
        total = own
        for k in range(nx - 1):
            total = total + sets[i][1][k].astype(F32)
        sets[i][2][...] = total
        sets[i][3][...] = total.astype(BF16)
        flights[i] = z_scatter(i)

    def x_sum_first(i):
        first, rows = pieces[i]
        size = rows // nx
        x_sum(i, g1_ref[pl.ds(pl.multiple_of(first + x * size, 16), size)])

    x_sum_first(0)
    land(y_out)
    total = mine2[rows_of(y, chunk)]
    for k in range(ny - 1):
        total = total + landed2[k].astype(F32)
    last = count - 1
    joined[:chunk] = total
    if joined.shape[0] > chunk:
        joined[chunk:] = jnp.zeros((joined.shape[0] - chunk, joined.shape[1]), F32)
    sets[last][0][...] = joined[...].astype(BF16)
    flights[last] = x_scatter(last)
    for i in range(1, count - 1):
        x_sum_first(i)
    x_sum(last, joined[rows_of(x, pieces[last][1] // nx)])

    order = [0, last] + list(range(1, count - 1))
    for i in order:
        size = pieces[i][1] // ns
        land(flights[i])
        done.extend(flights[i])
        total = sets[i][2][rows_of(z, size)]
        for k in range(nz - 1):
            total = total + sets[i][4][k].astype(F32)
        sets[i][5][rows_of(x * nz + z, size)] = total.astype(BF16)
        flights[i] = z_gather(i)
    for i in order:
        land(flights[i])
        done.extend(flights[i])
        flights[i] = x_gather(i)
    land(flights[last])
    done.extend(flights[last])
    done.extend(y_out)
    here = full2.at[pl.ds(pl.multiple_of(core * half + y * chunk, 16), chunk)]
    here[...] = sets[last][5][:chunk]
    y_back = start([
        remote(here, here, y_sems.at[2, k - 1], y_sems.at[3, k - 1], "freq", y_peer(k) * 2 + core)
        for k in range(1, ny)
    ])
    done.extend(y_back)
    for i in range(count - 1):
        first, size = pieces[i]
        land(flights[i])
        done.extend(flights[i])
        o1_ref[first : first + size] = sets[i][5][...].astype(F32)
    land(y_back)
    ours = full2.at[rows_of(core, half)]
    core_back = remote(ours, ours, core_sems.at[1, 0], core_sems.at[1, 1], "freq", partner)
    done += start([core_back])
    o2_ref[rows_of(core, half)] = ours[...].astype(F32)
    core_back.wait_recv()
    o2_ref[rows_of(1 - core, half)] = full2[rows_of(1 - core, half)].astype(F32)
    for copy in done:
        copy.wait_send()


def sum_call(g1, g2):
    nf, ns = lax.axis_size("freq"), lax.axis_size("sky")
    ny = nf // 2
    nz = 4 if ns % 4 == 0 else 1
    nx = ns // nz
    rows1, cols1 = g1.shape
    rows2, cols2 = g2.shape
    half, chunk = rows2 // 2, rows2 // nf
    last = -(-chunk // (16 * ns)) * 16 * ns
    cut = rows1 // 3
    pieces = [(i * cut, cut) for i in range(3)] + [(0, last)]
    vmem = pl.BlockSpec(memory_space=pltpu.VMEM)
    dma = pltpu.SemaphoreType.DMA
    buffers = []
    for i, (_, size) in enumerate(pieces):
        cols = cols1 if i < 3 else cols2
        buffers += [
            pltpu.VMEM((size, cols), BF16),
            pltpu.VMEM((nx - 1, size // nx, cols), BF16),
            pltpu.VMEM((size // nx, cols), F32),
            pltpu.VMEM((size // nx, cols), BF16),
            pltpu.VMEM((nz - 1, size // ns, cols), BF16),
            pltpu.VMEM((size, cols), BF16),
        ]
    return pl.pallas_call(
        functools.partial(sum_kernel, pieces, nx),
        out_shape=(
            jax.ShapeDtypeStruct((rows1, cols1), F32),
            jax.ShapeDtypeStruct((rows2, cols2), F32),
        ),
        in_specs=[vmem] * 2,
        out_specs=(vmem,) * 2,
        scratch_shapes=[
            pltpu.VMEM((half, cols2), BF16),
            pltpu.VMEM((half, cols2), BF16),
            pltpu.VMEM((half, cols2), F32),
            pltpu.VMEM((half, cols2), BF16),
            pltpu.VMEM((ny - 1, chunk, cols2), BF16),
            pltpu.VMEM((last, cols2), F32),
            pltpu.VMEM((rows2, cols2), BF16),
            dma((2, 2)),
            dma((4, ny - 1)),
            dma((4, 4, nx - 1)),
            dma((4, 4, nz - 1)),
        ]
        + buffers,
        compiler_params=pltpu.CompilerParams(
            collective_id=0, has_side_effects=True, vmem_limit_bytes=VMEM_LIMIT
        ),
        cost_estimate=pl.CostEstimate(flops=0, bytes_accessed=40 * g1.size, transcendentals=0),
    )(g1, g2)


def body(sky_cube, weight_first, weight_second, cotangent):
    strip, rows, _ = cotangent.shape
    weight_back = jnp.transpose(weight_second[::-1, ::-1], (0, 1, 3, 2))
    features, first, second = main_call(
        sky_cube, weight_first, weight_second, weight_back, cotangent
    )
    sum_first, sum_second = sum_call(
        first.reshape(-1, first.shape[3]), second.reshape(-1, second.shape[3])
    )
    grad_first = jnp.transpose(sum_first.reshape(first.shape), (0, 1, 3, 2))
    grad_second = jnp.transpose(sum_second.reshape(second.shape), (0, 1, 3, 2))
    return (features.reshape(strip, rows, -1), grad_first, grad_second)


def solution(mesh):
    return jax.shard_map(
        body,
        mesh=mesh,
        in_specs=(P(None, "sky", "freq"), P(None, None, "freq", None), P(), P("freq", "sky", None)),
        out_specs=(P("freq", "sky", None), P(None, None, "freq", None), P()),
        check_vma=False,
    )
```

```python
import functools

import jax
import jax.numpy as jnp
from jax import lax
from jax.experimental import pallas as pl
from jax.experimental.pallas import tpu as pltpu
from jax.sharding import PartitionSpec as P

MESH = pl.DeviceIdType.MESH
VMEM_LIMIT = 60 * 1024 * 1024
BLOCK = 16
F32 = jnp.float32
BF16 = jnp.bfloat16


def remote(src, dst, send, recv, axis, peer):
    return pltpu.make_async_remote_copy(
        src_ref=src,
        dst_ref=dst,
        send_sem=send,
        recv_sem=recv,
        device_id={axis: peer},
        device_id_type=MESH,
    )


def greet(targets):
    barrier = pltpu.get_barrier_semaphore()
    for axis, peer in targets:
        pl.semaphore_signal(barrier, inc=1, device_id={axis: peer}, device_id_type=MESH)
    pl.semaphore_wait(barrier, len(targets))


def take_edges(shifts, stage):
    rows = shifts.shape[2]

    def one(i, carry):
        c = pl.multiple_of(i * BLOCK, BLOCK)
        x = shifts[1, pl.ds(c, BLOCK)].astype(F32)
        stage[0, pl.ds(c, BLOCK)] = x[:, 0, :].astype(BF16)
        stage[1, pl.ds(c, BLOCK)] = x[:, rows - 1, :].astype(BF16)
        return carry

    lax.fori_loop(0, shifts.shape[1] // BLOCK, one, 0)


def row_copies(stage, halo, send, recv):
    sky = lax.axis_index("sky")
    down = remote(stage.at[0], halo.at[1], send.at[0], recv.at[1], "sky", sky - 1)
    up = remote(stage.at[1], halo.at[0], send.at[1], recv.at[0], "sky", sky + 1)
    return down, up


def send_rows(stage, halo, send, recv):
    sky, count = lax.axis_index("sky"), lax.axis_size("sky")
    down, up = row_copies(stage, halo, send, recv)

    @pl.when(sky > 0)
    def _():
        down.start()

    @pl.when(sky < count - 1)
    def _():
        up.start()

    @pl.when(sky == 0)
    def _():
        halo[0] = jnp.zeros(halo.shape[1:], halo.dtype)

    @pl.when(sky == count - 1)
    def _():
        halo[1] = jnp.zeros(halo.shape[1:], halo.dtype)


def land_rows(stage, halo, send, recv):
    sky, count = lax.axis_index("sky"), lax.axis_size("sky")
    down, up = row_copies(stage, halo, send, recv)

    @pl.when(sky > 0)
    def _():
        down.wait_send()
        up.wait_recv()

    @pl.when(sky < count - 1)
    def _():
        up.wait_send()
        down.wait_recv()


def column_copies(shifts, strip, send, recv):
    freq = lax.axis_index("freq")
    down = remote(shifts.at[1, 1], shifts.at[1, strip + 1], send.at[0], recv.at[1], "freq", freq - 1)
    up = remote(shifts.at[1, strip], shifts.at[1, 0], send.at[1], recv.at[0], "freq", freq + 1)
    return down, up


def send_columns(shifts, strip, send, recv):
    freq, count = lax.axis_index("freq"), lax.axis_size("freq")
    down, up = column_copies(shifts, strip, send, recv)
    line = jnp.zeros(shifts.shape[2:], shifts.dtype)

    @pl.when(freq > 0)
    def _():
        down.start()

    @pl.when(freq < count - 1)
    def _():
        up.start()

    @pl.when(freq == 0)
    def _():
        shifts[1, 0] = line

    @pl.when(freq == count - 1)
    def _():
        shifts[1, strip + 1] = line


def land_columns(shifts, strip, send, recv):
    freq, count = lax.axis_index("freq"), lax.axis_size("freq")
    down, up = column_copies(shifts, strip, send, recv)

    @pl.when(freq > 0)
    def _():
        down.wait_send()
        up.wait_recv()

    @pl.when(freq < count - 1)
    def _():
        up.wait_send()
        down.wait_recv()


def clear_tail(shifts, used):
    shifts[1, used:] = jnp.zeros((shifts.shape[1] - used,) + shifts.shape[2:], shifts.dtype)


def build_shifts(shifts, halo):
    rows, chans = shifts.shape[2:]
    step = BLOCK
    row = lax.broadcasted_iota(jnp.int32, (step, rows, chans), 1)

    def one(i, carry):
        c = pl.multiple_of(i * step, step)
        wide = shifts[1, pl.ds(c, step)].astype(F32)
        top = jnp.broadcast_to(halo[0, pl.ds(c, step)].astype(F32)[:, None, :], wide.shape)
        bot = jnp.broadcast_to(halo[1, pl.ds(c, step)].astype(F32)[:, None, :], wide.shape)
        up = jnp.where(row == 0, top, pltpu.roll(wide, 1, 1))
        down = jnp.where(row == rows - 1, bot, pltpu.roll(wide, rows - 1, 1))
        shifts[0, pl.ds(c, step)] = up.astype(BF16)
        shifts[2, pl.ds(c, step)] = down.astype(BF16)
        return carry

    lax.fori_loop(0, shifts.shape[1] // step, one, 0)


def conv_block(shifts, c, w_ref):
    rows, chans = shifts.shape[2:]
    pieces = [
        shifts[q, pl.ds(c + p, BLOCK)].reshape(BLOCK * rows, chans)
        for p in range(3)
        for q in range(3)
    ]
    return jnp.dot(
        jnp.concatenate(pieces, axis=1),
        w_ref[...].reshape(9 * chans, -1),
        preferred_element_type=F32,
    )


def add_grad(shifts, c, cols, d_ref, flipped, sums, after=None):
    rows, chans = shifts.shape[2:]
    span = cols * rows
    for k in range(span // 256):
        flipped[:, k * 256 : (k + 1) * 256] = d_ref[k * 256 : (k + 1) * 256].T
    outs = flipped.shape[0]
    for p in range(3):
        for q in range(3):
            piece = shifts[q, pl.ds(c + p, cols)].reshape(span, chans)
            at = (3 * p + q) * outs
            sums[at : at + outs] += jnp.dot(flipped[...], piece, preferred_element_type=F32)
        if after is not None:
            next(after)


def main_kernel(
    pieces, nx,
    x_hbm, w1_ref, w2_ref, w2b_ref, cot_ref,
    feat_ref, g1_ref, g2_ref,
    xs, cs, hs, xstage, xhalo, cstage, chalo, hstage, hhalo,
    give, got, part, mid, landed, own, back, dall, flipped,
    load_sem, row_send, row_recv, col_send, col_recv,
    give_send, give_recv, mid_send, mid_recv,
    far_send, far_recv, near_send, near_recv, pass_send, pass_recv, *sum_refs,
):
    freq, nf = lax.axis_index("freq"), lax.axis_size("freq")
    sky, ns = lax.axis_index("sky"), lax.axis_size("sky")
    ny = nf // 2
    y, core = freq // 2, freq % 2
    partner = y * 2 + 1 - core
    count, rows = x_hbm.shape[:2]
    strip = count // nf
    blocks = strip // BLOCK
    size = BLOCK * rows

    load = pltpu.make_async_copy(x_hbm, xs.at[1, pl.ds(1, count)], load_sem)
    load.start()
    xs[1, 0] = jnp.zeros(xs.shape[2:], BF16)
    clear_tail(xs, count + 1)
    clear_tail(cs, strip + 2)
    clear_tail(hs, strip + 2)
    cs[1, 1 : strip + 1] = cot_ref[...]
    greet(
        [("freq", lax.rem(freq + k, nf)) for k in range(1, nf)]
        + [("sky", lax.rem(sky + 1, ns)), ("sky", lax.rem(sky + ns - 1, ns))]
        + [("sky", sky // nx * nx + lax.rem(sky % nx + k, nx)) for k in range(1, nx)]
        + [("sky", lax.rem(sky + k * nx, ns)) for k in range(1, ns // nx)]
    )
    sums = sum_steps(pieces, nx, g1_ref, g2_ref, sum_refs)
    send_columns(cs, strip, col_send.at[0], col_recv.at[0])
    load.wait()
    take_edges(xs, xstage)
    send_rows(xstage, xhalo, row_send.at[0], row_recv.at[0])
    land_columns(cs, strip, col_send.at[0], col_recv.at[0])
    take_edges(cs, cstage)
    send_rows(cstage, chalo, row_send.at[1], row_recv.at[1])
    land_rows(xstage, xhalo, row_send.at[0], row_recv.at[0])
    build_shifts(xs, xhalo)

    def give_copy(t):
        return remote(
            give.at[t], got.at[t], give_send.at[t], give_recv.at[t], "freq", partner
        )

    def mid_copy(t):
        peer = lax.rem(y + 1 + t // blocks, ny) * 2 + core
        return remote(mid.at[t], landed.at[t], mid_send.at[t], mid_recv.at[t], "freq", peer)

    away = (ny - 1) * blocks
    steps = ny * blocks

    def one(t, carry):
        @pl.when(t < steps)
        def _():
            dest = lax.rem(y + 1 + t // blocks, ny) * 2
            sub = lax.rem(t, blocks) * BLOCK
            give[t] = conv_block(xs, (dest + 1 - core) * strip + sub, w1_ref).astype(BF16)
            give_copy(t).start()
            part[lax.rem(t, 2)] = conv_block(xs, (dest + core) * strip + sub, w1_ref)

        @pl.when(t > 0)
        def _():
            before = t - 1
            give_copy(before).wait_recv()
            total = part[lax.rem(before, 2)] + got[before].astype(F32)

            @pl.when(before < away)
            def _():
                mid[before] = total.astype(BF16)
                mid_copy(before).start()

            @pl.when(before >= away)
            def _():
                own[before - away] = total

        return carry

    lax.fori_loop(0, steps + 1, one, 0)

    land_rows(cstage, chalo, row_send.at[1], row_recv.at[1])
    build_shifts(cs, chalo)

    def one_back(i, carry):
        back[i] = conv_block(cs, i * BLOCK, w2b_ref)
        return carry

    lax.fori_loop(0, blocks, one_back, 0)

    def one_pre(i, carry):
        pre = own[i]
        for dy in range(ny - 1):
            mid_copy(dy * blocks + i).wait_recv()
            pre = pre + landed[dy * blocks + i].astype(F32)
        sigma = jax.nn.sigmoid(pre)
        hs[1, pl.ds(1 + i * BLOCK, BLOCK)] = (pre * sigma).astype(BF16).reshape(BLOCK, rows, -1)
        delta = back[i] * sigma * (1.0 + pre * (1.0 - sigma))
        dall[freq, pl.ds(pl.multiple_of(i * size, size), size)] = delta.astype(BF16)
        return carry

    lax.fori_loop(0, blocks, one_pre, 0)

    send_columns(hs, strip, col_send.at[1], col_recv.at[1])

    def far_copy(dy):
        peer = lax.rem(y + dy, ny) * 2 + core
        return remote(
            dall.at[freq], dall.at[freq], far_send.at[dy - 1], far_recv.at[dy - 1], "freq", peer
        )

    def pass_copy(dy):
        owner = lax.rem(y + ny - dy, ny) * 2 + core
        return remote(
            dall.at[owner], dall.at[owner], pass_send.at[dy - 1], pass_recv.at[dy - 1],
            "freq", partner,
        )

    near = remote(dall.at[freq], dall.at[freq], near_send, near_recv, "freq", partner)
    for dy in range(1, ny):
        far_copy(dy).start()
    near.start()
    land_columns(hs, strip, col_send.at[1], col_recv.at[1])
    take_edges(hs, hstage)
    send_rows(hstage, hhalo, row_send.at[2], row_recv.at[2])

    g1_ref[...] = jnp.zeros_like(g1_ref)
    g2_ref[...] = jnp.zeros_like(g2_ref)
    add_grad(xs, freq * strip, strip, dall.at[freq], flipped, g1_ref)
    land_rows(hstage, hhalo, row_send.at[2], row_recv.at[2])
    build_shifts(hs, hhalo)

    def one_feature(i, carry):
        value = conv_block(hs, i * BLOCK, w2_ref)
        feat_ref[pl.ds(pl.multiple_of(i * size, size), size)] = value.astype(feat_ref.dtype)
        return carry

    lax.fori_loop(0, blocks, one_feature, 0)
    near.wait_recv()
    add_grad(xs, partner * strip, strip, dall.at[partner], flipped, g1_ref)
    add_grad(hs, 0, strip, cot_ref.reshape(strip * rows, -1), flipped, g2_ref)
    next(sums)
    for dy in range(1, ny):
        far_copy(dy).wait_recv()
        pass_copy(dy).start()
        owner = lax.rem(y + ny - dy, ny) * 2
        add_grad(xs, (owner + core) * strip, strip, dall.at[owner + core], flipped, g1_ref)
    next(sums)
    for dy in range(1, ny):
        pass_copy(dy).wait_recv()
        owner = lax.rem(y + ny - dy, ny) * 2
        other = owner + 1 - core
        after = sums if dy == ny - 1 else None
        add_grad(xs, other * strip, strip, dall.at[other], flipped, g1_ref, after)
    for _ in sums:
        pass

    def drain(t, carry):
        give_copy(t).wait_send()

        @pl.when(t < away)
        def _():
            mid_copy(t).wait_send()

        return carry

    lax.fori_loop(0, steps, drain, 0)
    near.wait_send()
    for dy in range(1, ny):
        far_copy(dy).wait_send()
        pass_copy(dy).wait_send()


def main_call(x, w1, w2, w2b, cot):
    nf = lax.axis_size("freq")
    ny = nf // 2
    count, rows, chans = x.shape
    strip, _, outs = cot.shape
    hid = w1.shape[3]
    blocks = strip // BLOCK
    size = BLOCK * rows
    steps, away = ny * blocks, (ny - 1) * blocks
    wide, thin = count + BLOCK, strip + BLOCK
    vmem = pl.BlockSpec(memory_space=pltpu.VMEM)
    dma = pltpu.SemaphoreType.DMA
    ns = lax.axis_size("sky")
    nz = 4 if ns % 4 == 0 else 1
    nx = ns // nz
    half, chunk = 9 * outs // 2, 9 * outs // nf
    last = -(-chunk // (16 * ns)) * 16 * ns
    cut = 3 * hid
    pieces = [(i * cut, cut) for i in range(3)] + [(0, last)]
    buffers = []
    for i, (_, part) in enumerate(pieces):
        cols = chans if i < 3 else hid
        buffers += [
            pltpu.VMEM((part, cols), BF16),
            pltpu.VMEM((nx - 1, part // nx, cols), BF16),
            pltpu.VMEM((part // nx, cols), F32),
            pltpu.VMEM((part // nx, cols), BF16),
            pltpu.VMEM((nz - 1, part // ns, cols), BF16),
            pltpu.VMEM((part, cols), BF16),
        ]
    return pl.pallas_call(
        functools.partial(main_kernel, pieces, nx),
        out_shape=(
            jax.ShapeDtypeStruct((strip * rows, outs), BF16),
            jax.ShapeDtypeStruct((9 * hid, chans), F32),
            jax.ShapeDtypeStruct((9 * outs, hid), F32),
        ),
        in_specs=[pl.BlockSpec(memory_space=pl.ANY)] + [vmem] * 4,
        out_specs=(vmem,) * 3,
        scratch_shapes=[
            pltpu.VMEM((3, wide, rows, chans), BF16),
            pltpu.VMEM((3, thin, rows, outs), BF16),
            pltpu.VMEM((3, thin, rows, hid), BF16),
            pltpu.VMEM((2, wide, chans), BF16),
            pltpu.VMEM((2, wide, chans), BF16),
            pltpu.VMEM((2, thin, outs), BF16),
            pltpu.VMEM((2, thin, outs), BF16),
            pltpu.VMEM((2, thin, hid), BF16),
            pltpu.VMEM((2, thin, hid), BF16),
            pltpu.VMEM((steps, size, hid), BF16),
            pltpu.VMEM((steps, size, hid), BF16),
            pltpu.VMEM((2, size, hid), F32),
            pltpu.VMEM((away, size, hid), BF16),
            pltpu.VMEM((away, size, hid), BF16),
            pltpu.VMEM((blocks, size, hid), F32),
            pltpu.VMEM((blocks, size, hid), F32),
            pltpu.VMEM((nf, strip * rows, hid), BF16),
            pltpu.VMEM((hid, strip * rows), BF16),
            dma,
            dma((3, 2)), dma((3, 2)), dma((2, 2)), dma((2, 2)),
            dma((steps,)), dma((steps,)), dma((away,)), dma((away,)),
            dma((ny - 1,)), dma((ny - 1,)), dma, dma, dma((ny - 1,)), dma((ny - 1,)),
            pltpu.VMEM((half, hid), BF16),
            pltpu.VMEM((half, hid), BF16),
            pltpu.VMEM((half, hid), F32),
            pltpu.VMEM((half, hid), BF16),
            pltpu.VMEM((ny - 1, chunk, hid), BF16),
            pltpu.VMEM((last, hid), F32),
            pltpu.VMEM((9 * outs, hid), BF16),
            dma((2, 2)),
            dma((4, ny - 1)),
            dma((4, 4, nx - 1)),
            dma((4, 4, nz - 1)),
        ]
        + buffers,
        compiler_params=pltpu.CompilerParams(
            collective_id=1, has_side_effects=True, vmem_limit_bytes=VMEM_LIMIT
        ),
        cost_estimate=pl.CostEstimate(
            flops=36 * count * rows * chans * hid, bytes_accessed=4 * x.size, transcendentals=0
        ),
    )(x, w1, w2, w2b, cot)


def sum_steps(pieces, nx, g1_ref, g2_ref, refs):
    refs = list(refs)
    o1_ref, o2_ref = g1_ref, g2_ref
    freq, nf = lax.axis_index("freq"), lax.axis_size("freq")
    sky, ns = lax.axis_index("sky"), lax.axis_size("sky")
    ny, nz = nf // 2, ns // nx
    y, core = freq // 2, freq % 2
    z, x = sky // nx, sky % nx
    partner = y * 2 + 1 - core
    half = g2_ref.shape[0] // 2
    chunk = half // ny
    side, side_in, mine2, side_y, landed2, joined, full2 = refs[:7]
    core_sems, y_sems, x_sems, z_sems = refs[7:11]
    rest = refs[11:]
    sets = [rest[6 * i : 6 * i + 6] for i in range(len(pieces))]

    def rows_of(i, size):
        return pl.ds(pl.multiple_of(i * size, 16), size)

    def start(copies):
        for copy in copies:
            copy.start()
        return copies

    def land(copies):
        for copy in copies:
            copy.wait_recv()

    def x_peer(k):
        return z * nx + lax.rem(x + k, nx)

    def z_peer(k):
        return lax.rem(z + k, nz) * nx + x

    def y_peer(k):
        return lax.rem(y + k, ny)

    done = []
    side[...] = g2_ref[rows_of(1 - core, half)].astype(BF16)
    core_out = remote(side, side_in, core_sems.at[0, 0], core_sems.at[0, 1], "freq", partner)
    done += start([core_out])
    yield

    def x_scatter(i):
        src, land_x = sets[i][0], sets[i][1]
        size = pieces[i][1] // nx
        return start([
            remote(src.at[rows_of(lax.rem(x + k, nx), size)], land_x.at[k - 1],
                   x_sems.at[0, i, k - 1], x_sems.at[1, i, k - 1], "sky", x_peer(k))
            for k in range(1, nx)
        ])

    def z_scatter(i):
        mid, land_z = sets[i][3], sets[i][4]
        size = pieces[i][1] // ns
        return start([
            remote(mid.at[rows_of(lax.rem(z + k, nz), size)], land_z.at[k - 1],
                   z_sems.at[0, i, k - 1], z_sems.at[1, i, k - 1], "sky", z_peer(k))
            for k in range(1, nz)
        ])

    def z_gather(i):
        size = pieces[i][1] // ns
        here = sets[i][5].at[rows_of(x * nz + z, size)]
        return start([
            remote(here, here, z_sems.at[2, i, k - 1], z_sems.at[3, i, k - 1], "sky", z_peer(k))
            for k in range(1, nz)
        ])

    def x_gather(i):
        size = pieces[i][1] // nx
        here = sets[i][5].at[rows_of(x, size)]
        return start([
            remote(here, here, x_sems.at[2, i, k - 1], x_sems.at[3, i, k - 1], "sky", x_peer(k))
            for k in range(1, nx)
        ])

    count = len(pieces)
    flights = {}
    core_out.wait_recv()
    mine2[...] = g2_ref[rows_of(core, half)] + side_in[...].astype(F32)
    side_y[...] = mine2[...].astype(BF16)
    y_out = start([
        remote(side_y.at[rows_of(y_peer(k), chunk)],
               landed2.at[k - 1], y_sems.at[0, k - 1], y_sems.at[1, k - 1],
               "freq", y_peer(k) * 2 + core)
        for k in range(1, ny)
    ])
    yield
    for i in range(count - 1):
        first, size = pieces[i]
        sets[i][0][...] = g1_ref[first : first + size].astype(BF16)
        flights[i] = x_scatter(i)
        yield

    def x_sum(i, own):
        size = pieces[i][1] // nx
        land(flights[i])
        done.extend(flights[i])
        total = own
        for k in range(nx - 1):
            total = total + sets[i][1][k].astype(F32)
        sets[i][2][...] = total
        sets[i][3][...] = total.astype(BF16)
        flights[i] = z_scatter(i)

    def x_sum_first(i):
        first, rows = pieces[i]
        size = rows // nx
        x_sum(i, g1_ref[pl.ds(pl.multiple_of(first + x * size, 16), size)])

    land(y_out)
    total = mine2[rows_of(y, chunk)]
    for k in range(ny - 1):
        total = total + landed2[k].astype(F32)
    last = count - 1
    joined[:chunk] = total
    if joined.shape[0] > chunk:
        joined[chunk:] = jnp.zeros((joined.shape[0] - chunk, joined.shape[1]), F32)
    sets[last][0][...] = joined[...].astype(BF16)
    flights[last] = x_scatter(last)
    for i in range(count - 1):
        x_sum_first(i)
    x_sum(last, joined[rows_of(x, pieces[last][1] // nx)])

    order = [0, 1, last] + list(range(2, count - 1))
    for i in order:
        size = pieces[i][1] // ns
        land(flights[i])
        done.extend(flights[i])
        total = sets[i][2][rows_of(z, size)]
        for k in range(nz - 1):
            total = total + sets[i][4][k].astype(F32)
        sets[i][5][rows_of(x * nz + z, size)] = total.astype(BF16)
        flights[i] = z_gather(i)
    for i in order:
        land(flights[i])
        done.extend(flights[i])
        flights[i] = x_gather(i)
    land(flights[last])
    done.extend(flights[last])
    done.extend(y_out)
    here = full2.at[pl.ds(pl.multiple_of(core * half + y * chunk, 16), chunk)]
    here[...] = sets[last][5][:chunk]
    y_back = start([
        remote(here, here, y_sems.at[2, k - 1], y_sems.at[3, k - 1], "freq", y_peer(k) * 2 + core)
        for k in range(1, ny)
    ])
    done.extend(y_back)
    for i in range(count - 1):
        first, size = pieces[i]
        land(flights[i])
        done.extend(flights[i])
        o1_ref[first : first + size] = sets[i][5][...].astype(F32)
    land(y_back)
    ours = full2.at[rows_of(core, half)]
    core_back = remote(ours, ours, core_sems.at[1, 0], core_sems.at[1, 1], "freq", partner)
    done += start([core_back])
    o2_ref[rows_of(core, half)] = ours[...].astype(F32)
    core_back.wait_recv()
    o2_ref[rows_of(1 - core, half)] = full2[rows_of(1 - core, half)].astype(F32)
    for copy in done:
        copy.wait_send()


def body(sky_cube, weight_first, weight_second, cotangent):
    strip, rows, _ = cotangent.shape
    weight_back = jnp.transpose(weight_second[::-1, ::-1], (0, 1, 3, 2))
    features, first, second = main_call(
        sky_cube, weight_first, weight_second, weight_back, cotangent
    )
    grad_first = jnp.transpose(first.reshape(3, 3, -1, first.shape[1]), (0, 1, 3, 2))
    grad_second = jnp.transpose(second.reshape(3, 3, -1, second.shape[1]), (0, 1, 3, 2))
    return (features.reshape(strip, rows, -1), grad_first, grad_second)


def solution(mesh):
    return jax.shard_map(
        body,
        mesh=mesh,
        in_specs=(P(None, "sky", "freq"), P(None, None, "freq", None), P(), P("freq", "sky", None)),
        out_specs=(P("freq", "sky", None), P(None, None, "freq", None), P()),
        check_vma=False,
    )
```
